256 devices in a mesh: region: 16 (over y, x), block: 16 (over z, core).
Axes of the slice: x: 4, y: 4, z: 8, core: 2. Of those that a mesh axis runs over, the one named last changes fastest.
Arguments:
- gap_terms: float32 [16, 16, 1536, 128], P('region', 'block'), may hold values from -6 to 6
- rigid_loads: float32 [16, 16, 6, 128], P('region', 'block'), may hold values from -384 to 384
- dual_matrix: bfloat16 [16, 16, 1536, 1536], P('region', 'block'), as said below
- dirichlet_matrix: bfloat16 [16, 16, 1536, 1536], P('region', 'block'), as said below
- rigid_modes: float32 [16, 16, 6, 1536], P('region', 'block'), as said below
- coarse_rows: float32 [16, 16, 6, 1536], P('region', 'block'), as said below
- face_slot: int32 [16, 16, 4], P('region', 'block'), may hold values from 0 to 5, as said below
- glue_sign: int32 [16, 16, 1536], P('region', 'block'), may hold values from -1 to 1, as said below
Outputs:
- multiplier: float32 [16, 16, 1536, 128], P('region', 'block')
The draws below stay inside these ranges and needn't reach their ends.
Inputs may be any that keep to these rules, and one draw needn't show every extreme that they name: `face_slot`: for each subdomain, four different slots; the two slots left hold multipliers of the clamped boundary. Row i of a face and row i of the facing face of the neighbour are one constraint. `glue_sign`: each entry is -1 or 1; a multiplier shared by two subdomains has opposite signs on its two sides. `rigid_modes`: on a face shared by two subdomains both hold the same values, row by row. `coarse_rows`: the rows of this subdomain's 6 modes in a symmetric positive definite coarse operator of order 1536, which stands in for the inverse of G^T G, where G maps c to the field that rigid assembles from signed_modes^T c. `dual_matrix`: symmetric positive definite. `dirichlet_matrix`: symmetric positive definite.
All inputs are finite; a program needn't handle non-finite values.
Results may differ from the reference program's by a relative error of at most 0.0026.
Values sent between devices are 32-bit elements; how exact they have to be, the bound alone decides.
A program may use at most 64 MiB of HBM per device.

```python
import math
import jax
import jax.numpy as jnp
from jax import lax

FACE = 256
SLOTS = 6
MODES = 6
NRHS = 128
ITERS = 2
NL = 1536
NR = 16
NBK = 16
COARSE = 1536


def permute_slots(subkey):
    return jax.random.permutation(subkey, SLOTS)


def slot_layout(key):
    layout_key = jax.random.fold_in(key, 101)
    block_keys = jax.random.split(layout_key, NR * NBK)
    slot_order = jax.vmap(permute_slots)(block_keys)
    return slot_order.reshape(NR, NBK, SLOTS).astype(jnp.int32)


def place_roles(role_values, slot_order):
    inverse = jnp.argsort(slot_order, axis=-1)
    return jnp.take_along_axis(role_values, inverse[..., None], axis=2)


def glue_pattern(key):
    slot_order = slot_layout(key)
    sign_key = jax.random.fold_in(key, 202)
    sign_bits = 2 * jax.random.randint(sign_key, (4, NR, NBK, FACE), 0, 2) - 1
    role_values = jnp.stack([-jnp.roll(sign_bits[0], 1, axis=0), sign_bits[0], -jnp.roll(sign_bits[1], 1, axis=1), sign_bits[1], sign_bits[2], sign_bits[3]], axis=2)
    return place_roles(role_values, slot_order).reshape(NR, NBK, NL).astype(jnp.int32)


def modes_pattern(key):
    slot_order = slot_layout(key)
    mode_key = jax.random.fold_in(key, 303)
    values = jax.random.normal(mode_key, (4, NR, NBK, MODES, FACE), jnp.float32)
    role_values = jnp.stack([jnp.roll(values[0], 1, axis=0), values[0], jnp.roll(values[1], 1, axis=1), values[1], 0.4 * values[2], 0.4 * values[3]], axis=2)
    placed = place_roles(role_values.reshape(NR, NBK, SLOTS, MODES * FACE), slot_order)
    return placed.reshape(NR, NBK, SLOTS, MODES, FACE).transpose(0, 1, 3, 2, 4).reshape(NR, NBK, MODES, NL)


def spd_single(subkey, lowest, highest):
    noise_key, diag_key = jax.random.split(subkey, 2)
    noise = jax.random.normal(noise_key, (NL, NL), jnp.float32)
    coupled = (noise + noise.T) * (0.42 / math.sqrt(NL))
    diagonal = jnp.exp(jax.random.uniform(diag_key, (NL,), jnp.float32, math.log(lowest), math.log(highest)))
    indices = jnp.arange(NL)
    return jnp.where(indices[:, None] == indices[None, :], diagonal[:, None], coupled)


def draw_face_slot(key, part):
    slot_order = slot_layout(key)
    return slot_order[..., :4]


def draw_glue_sign(key, part):
    sign_values = glue_pattern(key)
    return sign_values


def draw_rigid_modes(key, part):
    mode_values = modes_pattern(key)
    return mode_values


def draw_coarse_rows(key, part):
    key = jax.random.fold_in(key, 4)
    noise_key, diag_key = jax.random.split(key, 2)
    base = 1.0 / (4.2 * FACE)
    noise = jax.random.normal(noise_key, (COARSE, COARSE), jnp.float32)
    coupled = (noise + noise.T) * (0.15 * base / math.sqrt(COARSE))
    diagonal = base * jax.random.uniform(diag_key, (COARSE,), jnp.float32, 0.8, 1.2)
    indices = jnp.arange(COARSE)
    matrix = jnp.where(indices[:, None] == indices[None, :], diagonal[:, None], coupled)
    return matrix.reshape(NR, NBK, MODES, COARSE)


def draw_dual_matrix(key, part):
    key = jax.random.fold_in(key, 5)

    def one_block(subkey):
        matrix = spd_single(subkey, 2.5, 8.0)
        return matrix.astype(jnp.bfloat16)
    blocks = lax.map(one_block, jax.random.split(key, NR * NBK))
    return blocks.reshape(NR, NBK, NL, NL)


def draw_dirichlet_matrix(key, part):
    key = jax.random.fold_in(key, 6)

    def one_block(subkey):
        matrix = spd_single(subkey, 2.0, 7.0)
        return matrix.astype(jnp.bfloat16)
    blocks = lax.map(one_block, jax.random.split(key, NR * NBK))
    return blocks.reshape(NR, NBK, NL, NL)


def shard_levels(stream_key, dims, pieces, smallest, largest):
    loudness, own = 1.0, jax.random.fold_in(stream_key, 6)
    for position, blocks in pieces:
        heights = jnp.exp(jax.random.uniform(jax.random.fold_in(own, position), (blocks,), jnp.float32, smallest / len(pieces), largest / len(pieces)))
        loudness = loudness * jnp.repeat(heights, dims[position] // blocks).reshape([-1 if axis == position else 1 for axis in range(len(dims))])
    return loudness


def gaussian(stream_key, extent, spread, limit, shards=(), held_as=jnp.bfloat16):
    values = jax.random.normal(stream_key, extent, jnp.float32) * spread
    if len(shards) > 0:
        values = shard_levels(stream_key, extent, shards, -0.22, 0.18) * values
    return jnp.clip(values, min=-limit, max=limit).astype(held_as)


def setup_inputs(seed: int = 0) -> dict:
    splits = jax.random.split(jax.random.key(seed), 9)
    return {
        "gap_terms": gaussian(splits[0], (NR, NBK, NL, NRHS), 1.0, 6.0, ((0, 16), (1, 16)), jnp.float32),
        "rigid_loads": gaussian(splits[1], (NR, NBK, MODES, NRHS), (max(FACE // 4, 1)), 384.0, ((0, 16), (1, 16)), jnp.float32),
        "dual_matrix": draw_dual_matrix(jax.random.fold_in(splits[8], 71), 0),
        "dirichlet_matrix": draw_dirichlet_matrix(jax.random.fold_in(splits[8], 71), 0),
        "rigid_modes": draw_rigid_modes(jax.random.fold_in(splits[8], 71), 0),
        "coarse_rows": draw_coarse_rows(jax.random.fold_in(splits[8], 71), 0),
        "face_slot": draw_face_slot(jax.random.fold_in(splits[8], 71), 0),
        "glue_sign": draw_glue_sign(jax.random.fold_in(splits[8], 71), 0),
    }


precise = lax.Precision.HIGHEST


def grid_weights(face_slot):
    region_pos = jnp.arange(NR)[:, None] + jnp.zeros((1, NBK), jnp.int32)
    block_pos = jnp.zeros((NR, 1), jnp.int32) + jnp.arange(NBK)[None, :]
    present = jnp.stack([region_pos > 0, region_pos < NR - 1, block_pos > 0, block_pos < NBK - 1], axis=-1)
    positions = jnp.arange(NL) // FACE
    hits = (positions[None, None, None, :] == face_slot[..., None]) & present[..., None]
    return jnp.where(jnp.any(hits, axis=2), 0.5, 1.0).astype(jnp.float32)[..., None]


def assemble(contrib, face_slot):
    slot_parts = contrib.reshape(NR, NBK, SLOTS, FACE, NRHS)
    onehot = (face_slot[..., None] == jnp.arange(SLOTS)[None, None, None, :]).astype(jnp.float32)
    face_parts = jnp.einsum("rbds,rbsfn->rbdfn", onehot, slot_parts, precision=precise)
    zero_rows = jnp.zeros_like(face_parts[:1, :, 0])
    from_lower = jnp.concatenate([zero_rows, face_parts[:-1, :, 1]], axis=0)
    from_upper = jnp.concatenate([face_parts[1:, :, 0], zero_rows], axis=0)
    zero_cols = jnp.zeros_like(face_parts[:, :1, 0])
    from_before = jnp.concatenate([zero_cols, face_parts[:, :-1, 3]], axis=1)
    from_after = jnp.concatenate([face_parts[:, 1:, 2], zero_cols], axis=1)
    incoming = jnp.stack([from_lower, from_upper, from_before, from_after], axis=2)
    gathered_sum = jnp.einsum("rbds,rbdfn->rbsfn", onehot, incoming, precision=precise)
    return contrib + gathered_sum.reshape(contrib.shape)


def signed_product(matrices, glue_float, vectors):
    flat_blocks = matrices.reshape(NR * NBK, NL, NL)
    lowered = (glue_float * vectors).astype(jnp.bfloat16).reshape(NR * NBK, NL, NRHS)

    def product_one(operands):
        return jnp.dot(operands[0], operands[1], preferred_element_type=jnp.float32)

    result = lax.map(product_one, (flat_blocks, lowered)).reshape(NR, NBK, NL, NRHS)
    return glue_float * result


def coarse_coeffs(signed_modes, vectors):
    return jnp.einsum("rbki,rbin->rbkn", signed_modes, vectors, precision=precise)


def rigid_field(signed_modes, coarse_rows, coeffs, face_slot):
    stacked = coeffs.reshape(COARSE, NRHS)
    amplitude = jnp.einsum("rbkc,cn->rbkn", coarse_rows, stacked, precision=precise)
    contrib = jnp.einsum("rbki,rbkn->rbin", signed_modes, amplitude, precision=precise)
    return assemble(contrib, face_slot)


def inner_product(weights, left_side, right_side):
    return jnp.sum(weights * left_side * right_side, axis=(0, 1, 2))


def reference(gap_terms, rigid_loads, dual_matrix, dirichlet_matrix, rigid_modes, coarse_rows, face_slot, glue_sign):
    glue_float = glue_sign.astype(jnp.float32)[..., None]
    signed_modes = rigid_modes * glue_sign.astype(jnp.float32)[:, :, None, :]
    weights = grid_weights(face_slot)
    multiplier = rigid_field(signed_modes, coarse_rows, rigid_loads, face_slot)
    residual = assemble(gap_terms - signed_product(dual_matrix, glue_float, multiplier), face_slot)
    search = residual - rigid_field(signed_modes, coarse_rows, coarse_coeffs(signed_modes, residual), face_slot)
    direction = search
    energy_last = inner_product(weights, search, search)
    for iteration in range(ITERS):
        precond = assemble(weights * signed_product(dirichlet_matrix, glue_float, weights * search), face_slot)
        projected = precond - rigid_field(signed_modes, coarse_rows, coarse_coeffs(signed_modes, precond), face_slot)
        energy_now = inner_product(weights, search, projected)
        if iteration == 0:
            direction = projected
        else:
            direction = projected + (energy_now / energy_last) * direction
        operated = assemble(signed_product(dual_matrix, glue_float, direction), face_slot)
        curvature = inner_product(weights, direction, operated)
        step_size = energy_now / curvature
        multiplier = multiplier + step_size * direction
        residual = residual - step_size * operated
        search = residual - rigid_field(signed_modes, coarse_rows, coarse_coeffs(signed_modes, residual), face_slot)
        energy_last = energy_now
    return multiplier
```

```python
import jax
import jax.numpy as jnp
from jax import lax
from jax.experimental import pallas as pl
from jax.experimental.pallas import tpu as pltpu
from jax.sharding import PartitionSpec as P

FACE = 256
SLOTS = 6
NL = FACE * SLOTS
NRHS = 128
NR = 16
NBK = 16
ROUNDS = 5

f32 = jnp.float32
bf16 = jnp.bfloat16
MESH = pl.DeviceIdType.MESH


def split(x):
    hi = x.astype(bf16)
    lo = (x - hi.astype(f32)).astype(bf16)
    return hi, lo


def dot(a, b):
    return jnp.dot(a, b, preferred_element_type=f32)


def kernel(
    slot_ref, gap_hbm, loads_ref, dual_hbm, diri_hbm, modes_ref, coarse_ref, glue_ref,
    out_ref,
    dmat, emat, gap_v, glue_b, m16, mt, coarse8, kown, kown16, kdist, khi, klo,
    lam, search, direc, wloc, field, low, pbuf, xbuf, abuf,
    g1_out, g1_in, g1_all, s1_out, s1_in, s2_out, s2_in, s3_out, s3_in,
    a_out, al_all, face_out, face_in, f_out, f_in,
    load_sem, kd_send, kd_recv, st_send, st_recv, a_send, a_recv, fc_send, fc_recv,
):
    region = lax.axis_index("region")
    block = lax.axis_index("block")
    present = [region > 0, region < NR - 1, block > 0, block < NBK - 1]
    peer = [
        {"region": region - 1}, {"region": region + 1},
        {"block": block - 1}, {"block": block + 1},
    ]

    def rows8(index):
        return pl.ds(pl.multiple_of(index * 8, 8), 8)

    loads = [
        pltpu.make_async_copy(gap_hbm, gap_v, load_sem.at[0]),
        pltpu.make_async_copy(dual_hbm, dmat, load_sem.at[1]),
        pltpu.make_async_copy(diri_hbm, emat, load_sem.at[2]),
    ]
    for copy in loads:
        copy.start()

    for ref in al_all:
        ref[...] = jnp.zeros_like(ref)
    for ref in face_in:
        ref[4] = jnp.zeros((FACE, NRHS), f32)
    for f in range(4):
        @pl.when(jnp.logical_not(present[f]))
        def _():
            for ref in face_in:
                ref[f] = jnp.zeros((FACE, NRHS), f32)

    barrier = pltpu.get_barrier_semaphore()

    def greet(p, carry):
        pl.semaphore_signal(
            barrier, inc=1, device_id={"block": lax.rem(block + p, NBK)}, device_id_type=MESH
        )
        pl.semaphore_signal(
            barrier, inc=1, device_id={"region": lax.rem(region + p, NR)}, device_id_type=MESH
        )
        return carry

    lax.fori_loop(1, 16, greet, 0)

    g1_out[...] = jnp.zeros_like(g1_out)
    g1_out[0:6, :] = loads_ref[...]
    coarse8[...] = jnp.zeros_like(coarse8)
    coarse8[0:6, :] = coarse_ref[...]
    row_i = lax.broadcasted_iota(jnp.int32, (96, 128), 0)
    lane_i = lax.broadcasted_iota(jnp.int32, (96, 128), 1)
    spread = ((row_i == (lane_i >> 3) * 6 + (lane_i & 7)) & ((lane_i & 7) < 6)).astype(f32)
    row_8 = lax.broadcasted_iota(jnp.int32, (8, 128), 0)
    lane_8 = lax.broadcasted_iota(jnp.int32, (8, 128), 1)
    lane_blk = lane_8 >> 3
    passing = ((row_8 >= 6) & ((lane_8 & 7) == row_8)).astype(f32)
    for r in range(NR):
        piece = coarse8[:, 96 * r:96 * r + 96]
        wide = jnp.dot(piece, spread, preferred_element_type=f32, precision=lax.Precision.HIGHEST)
        kown[r] = wide + passing
    pl.semaphore_wait(barrier, 30)

    def all_to(axis, me, count, src, dst, send_sem, recv_sem):
        def one(p, carry):
            to = lax.rem(me + p, count)
            pltpu.make_async_remote_copy(
                src_ref=src(to), dst_ref=dst.at[me], send_sem=send_sem, recv_sem=recv_sem,
                device_id={axis: to}, device_id_type=MESH,
            ).start()
            return carry

        lax.fori_loop(1, count, one, 0)

    def await_all(dst, sem):
        part = dst.at[pl.ds(0, 15)]
        pltpu.make_async_copy(part, part, sem).wait()

    all_to("block", block, NBK, lambda to: g1_out, g1_in, st_send.at[0, 0], st_recv.at[0, 0])
    all_to("block", block, NBK, lambda to: kown, kdist, kd_send, kd_recv)
    g1_in[block] = g1_out[...]
    kdist[block] = kown[...]
    for r in range(NR):
        piece = kown[r]
        hi = piece.astype(bf16).astype(f32)
        kown16[:, 128 * r:128 * r + 128] = jnp.concatenate([hi, piece - hi], axis=0).astype(bf16)

    for i in range(NL // 128):
        signs = glue_ref[0:1, 128 * i:128 * i + 128].astype(f32)
        glue_b[128 * i:128 * i + 128, :] = jnp.broadcast_to(signs, (128, 128)).T
        signed = jnp.concatenate(
            [modes_ref[:, 128 * i:128 * i + 128] * signs, jnp.zeros((2, 128), f32)], axis=0
        )
        hi = signed.astype(bf16).astype(f32)
        m16[:, 128 * i:128 * i + 128] = jnp.concatenate([hi, signed - hi], axis=0).astype(bf16)
        stacked = jnp.concatenate(
            [hi, hi, signed - hi, jnp.zeros((104, 128), f32)], axis=0
        ).T
        mt[128 * i:128 * i + 128, :] = stacked[:, 0:32].astype(bf16)

    facing = []
    share = []
    for j in range(SLOTS):
        where = jnp.int32(4)
        weight = jnp.float32(1.0)
        for f in range(4):
            hit = slot_ref[0, f] == j
            where = jnp.where(hit, f, where)
            weight = jnp.where(jnp.logical_and(hit, present[f]), 0.5, weight)
        facing.append(where)
        share.append(weight)

    def swap_amplitudes(k, others):
        for f in others:
            @pl.when(present[f])
            def _(f=f):
                pltpu.make_async_remote_copy(
                    src_ref=a_out.at[k], dst_ref=al_all[k].at[f ^ 1],
                    send_sem=a_send.at[k, f], recv_sem=a_recv.at[k, f ^ 1],
                    device_id=peer[f], device_id_type=MESH,
                ).start()

    def amplitude_done(k, others):
        for f in others:
            @pl.when(present[f])
            def _(f=f):
                pltpu.make_async_copy(a_out.at[k], al_all[k].at[f], a_recv.at[k, f]).wait()

    def field_slot(k, j):
        q = a_out[k] - al_all[k][facing[j]]
        hi = q.astype(bf16).astype(f32)
        stacked = jnp.concatenate([hi, q - hi, hi, jnp.zeros_like(q)], axis=0).astype(bf16)
        return dot(mt[FACE * j:FACE * j + FACE, :], stacked)

    def product(matrix, j):
        rows = slice(FACE * j, FACE * j + FACE)
        return glue_b[rows, :] * dot(matrix[rows, :], low[...])

    def lower(j, value):
        rows = slice(FACE * j, FACE * j + FACE)
        low[rows, :] = (glue_b[rows, :] * value).astype(bf16)

    await_all(g1_in, st_recv.at[0, 0])
    all_to("region", region, NR, lambda to: g1_in, g1_all, st_send.at[0, 1], st_recv.at[0, 1])
    g1_all[region] = g1_in[...]
    await_all(g1_all, st_recv.at[0, 1])
    total = jnp.zeros((16, NRHS), f32)
    for r in range(0, NR, 2):
        pair = g1_all[r:r + 2].reshape(256, NRHS)
        hi, lo = split(pair)
        rows = kown16[:, 128 * r:128 * r + 256]
        total = total + (dot(rows, hi) + dot(rows, lo))
    a_out[0] = total[:8] + total[8:]
    swap_amplitudes(0, range(4))
    loads[0].wait()
    loads[1].wait()
    amplitude_done(0, range(4))
    for j in range(SLOTS):
        value = field_slot(0, j)
        lam[j] = value
        lower(j, value)
    for j in range(SLOTS):
        wloc[j] = gap_v[FACE * j:FACE * j + FACE, :] - product(dmat, j)

    xbuf[...] = jnp.zeros_like(xbuf)

    def coarse_round(k, extra, prepare=None):
        mine = extra
        for j in range(SLOTS):
            hi, lo = split(wloc[j])
            rows = m16[:, FACE * j:FACE * j + FACE]
            part = dot(rows, hi) + dot(rows, lo)
            part = part[:8] + part[8:]
            pbuf[j] = part
            mine = part if mine is None else mine + part
        xbuf[rows8(block), :] = mine
        place = [lax.rem(block + 8, 16), lax.rem(block + 9, 16), block - 1, block + 1]
        for f in range(4):
            part = pbuf[slot_ref[0, f]]

            @pl.when(present[f])
            def _(f=f, part=part):
                xbuf[rows8(place[f]), :] = -part
        s1_out[k] = xbuf[...].T.reshape(16, 8, 128)
        all_to(
            "block", block, NBK, lambda to: s1_out.at[k, to], s1_in.at[k],
            st_send.at[k, 0], st_recv.at[k, 0],
        )
        s1_in[k, block] = s1_out[k, block]
        for f in range(4):
            face_out[k - 1, f] = wloc[slot_ref[0, f]]
        await_all(s1_in.at[k], st_recv.at[k, 0])
        main = jnp.zeros((8, 128), f32)
        before = jnp.zeros((8, 128), f32)
        after = jnp.zeros((8, 128), f32)
        for t in range(NBK):
            tile = s1_in[k, t]
            main = main + jnp.where((lane_blk >= t - 1) & (lane_blk <= t + 1), tile, 0.0)
            before = before + jnp.where(lane_blk == (t + 8) % 16, tile, 0.0)
            after = after + jnp.where(lane_blk == (t + 9) % 16, tile, 0.0)
        s2_out[k, 0] = main
        s2_out[k, 1] = pltpu.roll(before, 64, 1)
        s2_out[k, 2] = pltpu.roll(after, 56, 1)
        all_to(
            "region", region, NR, lambda to: s2_out.at[k], s2_in.at[k],
            st_send.at[k, 1], st_recv.at[k, 1],
        )
        s2_in[k, region] = s2_out[k]
        for f in range(4):
            @pl.when(present[f])
            def _(f=f):
                pltpu.make_async_remote_copy(
                    src_ref=face_out.at[k - 1, f], dst_ref=face_in[k - 1].at[f ^ 1],
                    send_sem=fc_send.at[k - 1, f], recv_sem=fc_recv.at[k - 1, f ^ 1],
                    device_id=peer[f], device_id_type=MESH,
                ).start()
        if prepare is not None:
            prepare()
        await_all(s2_in.at[k], st_recv.at[k, 1])
        pieces = []
        for r in range(NR):
            tile = s2_in[k, r, 0]
            if r < NR - 1:
                tile = tile + s2_in[k, r + 1, 1]
            if r > 0:
                tile = tile + s2_in[k, r - 1, 2]
            hi = tile.astype(bf16).astype(f32)
            pieces.append(jnp.concatenate([hi, tile - hi], axis=0).astype(bf16))
        left = jnp.concatenate(pieces, axis=1)
        both = dot(left, khi[...]) + dot(left, klo[...])
        s3_out[k] = both[:8] + both[8:]
        all_to(
            "block", block, NBK, lambda to: s3_out.at[k], s3_in.at[k],
            st_send.at[k, 2], st_recv.at[k, 2],
        )
        s3_in[k, block] = s3_out[k]
        await_all(s3_in.at[k], st_recv.at[k, 2])
        abuf[...] = s3_in[k].reshape(128, 128).T
        a_out[k] = abuf[rows8(block), :]
        swap_amplitudes(k, range(2))
        for f, near in ((2, block - 1), (3, block + 1)):
            @pl.when(present[f])
            def _(f=f, near=near):
                al_all[k][f] = abuf[rows8(near), :]
        for f in range(4):
            @pl.when(present[f])
            def _(f=f):
                pltpu.make_async_copy(
                    face_out.at[k - 1, f], face_in[k - 1].at[f], fc_recv.at[k - 1, f]
                ).wait()
        amplitude_done(k, range(2))

    def assembled(k, j):
        return wloc[j] + face_in[k - 1][facing[j]] - field_slot(k, j)

    def inner(total, left, right):
        return total + jnp.sum((left * right).reshape(FACE // 8, 8, NRHS), axis=0)

    def finish(total):
        return jnp.sum(total, axis=0, keepdims=True)

    zero8 = jnp.zeros((8, NRHS), f32)

    def coarse_matrix():
        part = kdist.at[pl.ds(0, 15)]
        pltpu.make_async_copy(part, part, kd_recv).wait()
        for r in range(NR):
            hi, lo = split(kdist[:, r].reshape(128, 128).T)
            khi[128 * r:128 * r + 128, :] = hi
            klo[128 * r:128 * r + 128, :] = lo

    coarse_round(1, None, coarse_matrix)
    for j in range(SLOTS):
        value = assembled(1, j)
        search[j] = value
        lower(j, share[j] * value)
    loads[2].wait()
    for j in range(SLOTS):
        wloc[j] = share[j] * product(emat, j)

    coarse_round(2, None)
    energy = zero8
    for j in range(SLOTS):
        value = assembled(2, j)
        direc[j] = value
        lower(j, value)
        energy = inner(energy, share[j] * search[j], value)
    curvature = zero8
    for j in range(SLOTS):
        value = product(dmat, j)
        wloc[j] = value
        field[j] = value
        curvature = inner(curvature, direc[j], value)

    sums = jnp.concatenate([jnp.zeros((6, NRHS), f32), finish(energy), finish(curvature)], axis=0)
    coarse_round(3, sums)
    energy0 = a_out[3, 6:7, :]
    curvature0 = a_out[3, 7:8, :]
    step0 = energy0 / curvature0
    for j in range(SLOTS):
        value = search[j] - step0 * assembled(3, j)
        search[j] = value
        lower(j, share[j] * value)
    for j in range(SLOTS):
        wloc[j] = share[j] * product(emat, j)

    coarse_round(4, None)
    energy = zero8
    cross = zero8
    for j in range(SLOTS):
        value = assembled(4, j)
        lower(j, value)
        energy = inner(energy, share[j] * search[j], value)
        cross = inner(cross, value, field[j])
        search[j] = value
    curvature = zero8
    for j in range(SLOTS):
        curvature = inner(curvature, search[j], product(dmat, j))
    f_out[0] = jnp.concatenate(
        [finish(energy), finish(curvature), finish(cross), jnp.zeros((5, NRHS), f32)], axis=0
    )
    for stage, (axis, me) in enumerate((("block", block), ("region", region))):
        all_to(
            axis, me, 16, lambda to: f_out.at[stage], f_in.at[stage],
            st_send.at[5, stage], st_recv.at[5, stage],
        )
        f_in[stage, me] = f_out[stage]
        await_all(f_in.at[stage], st_recv.at[5, stage])
        f_out[stage + 1] = jnp.sum(f_in[stage], axis=0)
    energy1 = f_out[2, 0:1, :]
    beta = energy1 / energy0
    curvature1 = f_out[2, 1:2, :] + 2.0 * beta * f_out[2, 2:3, :] + beta * beta * curvature0
    step1 = energy1 / curvature1
    first = step0 + step1 * beta
    for j in range(SLOTS):
        out_ref[FACE * j:FACE * j + FACE, :] = lam[j] + first * direc[j] + step1 * search[j]

    def sent(ref, sem):
        pltpu.make_async_copy(ref, ref, sem).wait()

    sent(g1_in.at[pl.ds(0, 15)], st_send.at[0, 0])
    sent(g1_all.at[pl.ds(0, 15)], st_send.at[0, 1])
    sent(kdist.at[pl.ds(0, 15)], kd_send)
    for k in range(1, ROUNDS):
        sent(s1_in.at[k, pl.ds(0, 15)], st_send.at[k, 0])
        sent(s2_in.at[k, pl.ds(0, 15)], st_send.at[k, 1])
        sent(s3_in.at[k, pl.ds(0, 15)], st_send.at[k, 2])
    for stage in range(2):
        sent(f_in.at[stage, pl.ds(0, 15)], st_send.at[5, stage])
    for f in range(4):
        @pl.when(present[f])
        def _(f=f):
            for k in range(4):
                sent(face_out.at[k, f], fc_send.at[k, f])
            for k in range(ROUNDS):
                if k == 0 or f < 2:
                    sent(a_out.at[k], a_send.at[k, f])


def body(
    gap_terms, rigid_loads, dual_matrix, dirichlet_matrix, rigid_modes, coarse_rows,
    face_slot, glue_sign,
):
    vmem = pl.BlockSpec(memory_space=pltpu.VMEM)
    hbm = pl.BlockSpec(memory_space=pl.ANY)
    V = pltpu.VMEM
    slots = (SLOTS, FACE, NRHS)
    scratch = [
        V((NL, NL), bf16), V((NL, NL), bf16), V((NL, NRHS), f32), V((NL, NRHS), f32),
        V((16, NL), bf16), V((NL, 32), bf16), V((8, NL), f32),
        V((NR, 8, 128), f32), V((16, NR * 128), bf16), V((NBK, NR, 8, 128), f32),
        V((NR * 128, 128), bf16), V((NR * 128, 128), bf16),
        V(slots, f32), V(slots, f32), V(slots, f32), V(slots, f32), V(slots, f32),
        V((NL, NRHS), bf16), V((SLOTS, 8, NRHS), f32), V((128, 128), f32), V((128, 128), f32),
        V((8, 128), f32), V((NBK, 8, 128), f32), V((NR, NBK, 8, 128), f32),
        V((ROUNDS, NBK, 8, 128), f32), V((ROUNDS, NBK, 8, 128), f32),
        V((ROUNDS, 3, 8, 128), f32), V((ROUNDS, NR, 3, 8, 128), f32),
        V((ROUNDS, 8, 128), f32), V((ROUNDS, NBK, 8, 128), f32),
        V((ROUNDS, 8, 128), f32), tuple(V((5, 8, 128), f32) for _ in range(ROUNDS)),
        V((4, 4, FACE, NRHS), f32), tuple(V((5, FACE, NRHS), f32) for _ in range(4)),
        V((3, 8, 128), f32), V((2, 16, 8, 128), f32),
        pltpu.SemaphoreType.DMA((3,)), pltpu.SemaphoreType.DMA, pltpu.SemaphoreType.DMA,
        pltpu.SemaphoreType.DMA((ROUNDS + 1, 3)), pltpu.SemaphoreType.DMA((ROUNDS + 1, 3)),
        pltpu.SemaphoreType.DMA((ROUNDS, 4)), pltpu.SemaphoreType.DMA((ROUNDS, 4)),
        pltpu.SemaphoreType.DMA((4, 4)), pltpu.SemaphoreType.DMA((4, 4)),
    ]
    result = pl.pallas_call(
        kernel,
        out_shape=jax.ShapeDtypeStruct((NL, NRHS), f32),
        in_specs=[
            pl.BlockSpec(memory_space=pltpu.SMEM), hbm, vmem, hbm, hbm, vmem, vmem, vmem,
        ],
        out_specs=vmem,
        scratch_shapes=scratch,
        compiler_params=pltpu.CompilerParams(
            collective_id=0, has_side_effects=True, vmem_limit_bytes=48 * 1024 * 1024,
        ),
        cost_estimate=pl.CostEstimate(
            flops=5 * 2 * NL * NL * NRHS, bytes_accessed=12 * 1024 * 1024, transcendentals=0
        ),
    )(
        face_slot[0], gap_terms[0, 0], rigid_loads[0, 0], dual_matrix[0, 0],
        dirichlet_matrix[0, 0], rigid_modes[0, 0], coarse_rows[0, 0], glue_sign[0],
    )
    return result[None, None]


def solution(mesh):
    matrix = P("region", "block", None, None)
    vector = P("region", "block", None)
    return jax.shard_map(
        body, mesh=mesh, in_specs=(matrix,) * 6 + (vector,) * 2, out_specs=matrix,
        check_vma=False,
    )
```

```python
import jax
import jax.numpy as jnp
from jax import lax
from jax.experimental import pallas as pl
from jax.experimental.pallas import tpu as pltpu
from jax.sharding import PartitionSpec as P

FACE = 256
SLOTS = 6
NL = FACE * SLOTS
NRHS = 128
NR = 16
NBK = 16
FAR_FIRST = (8, 7, 9, 6, 10, 5, 11, 4, 12, 3, 13, 2, 14, 1, 15)
ROUNDS = 5

f32 = jnp.float32
bf16 = jnp.bfloat16
MESH = pl.DeviceIdType.MESH


def split(x):
    hi = x.astype(bf16)
    lo = (x - hi.astype(f32)).astype(bf16)
    return hi, lo


def dot(a, b):
    return jnp.dot(a, b, preferred_element_type=f32)


def kernel(
    gap_hbm, loads_hbm, dual_hbm, diri_hbm, modes_hbm, coarse_hbm, slot_arg, glue_hbm,
    out_ref,
    loads_ref, modes_ref, coarse_ref, glue_ref,
    dmat, emat, gap_v, glue_b, m16, u16, mt, coarse8, coarse_sib, kpair, kown, kdist, khi, klo,
    dcoef, ecoef, gcoef, ybuf, lown, ldist, lmat, lhi, llo, t_in,
    lam, search, direc, wloc, field, low, pbuf, xbuf, abuf,
    g1_in, g1_all, half_out, half_in, s1_out, s1_in, s2_out, s2_in, s3_out, s3_in,
    a_out, al_all, al_near, part, corr, face_out, face_in, f_out, f_in, c_out, c_in,
    load_sem, kd_send, kd_recv, ld_send, ld_recv, t_send, t_recv, sib_send, sib_recv, st_send, st_recv, a_send, a_recv, fc_send, fc_recv,
):
    region = lax.axis_index("region")
    block = lax.axis_index("block")
    present = [region > 0, region < NR - 1, block > 0, block < NBK - 1]
    peer = [
        {"region": region - 1}, {"region": region + 1},
        {"block": block - 1}, {"block": block + 1},
    ]

    def rows8(index):
        return pl.ds(pl.multiple_of(index * 8, 8), 8)

    slot_ref = slot_arg.at[0]
    core = lax.rem(block, 2)
    place = [lax.rem(block + 8, 16), lax.rem(block + 9, 16), block - 1, block + 1]
    sibling = {"block": block + 1 - 2 * core}
    barrier = pltpu.get_barrier_semaphore()
    for p in range(1, 16):
        pl.semaphore_signal(
            barrier, inc=1, device_id={"block": lax.rem(block + p, NBK)}, device_id_type=MESH
        )
        pl.semaphore_signal(
            barrier, inc=1, device_id={"region": lax.rem(region + p, NR)}, device_id_type=MESH
        )

    loads = [
        pltpu.make_async_copy(source, target, load_sem.at[i])
        for i, (source, target) in enumerate((
            (loads_hbm.at[0], loads_ref), (coarse_hbm.at[0], coarse_ref),
            (glue_hbm.at[0], glue_ref), (modes_hbm.at[0], modes_ref),
            (gap_hbm.at[0, 0], gap_v), (dual_hbm.at[0, 0], dmat), (diri_hbm.at[0, 0], emat),
        ))
    ]
    for copy in loads:
        copy.start()

    pending = []

    def send(src, dst, send_sem, recv_sem, target):
        pltpu.make_async_remote_copy(
            src_ref=src, dst_ref=dst, send_sem=send_sem, recv_sem=recv_sem,
            device_id=target, device_id_type=MESH,
        ).start()

    def all_to(axis, me, src, dst, send_sem, recv_sem):
        for p in FAR_FIRST:
            to = lax.rem(me + p, 16)
            send(src(to), dst.at[me], send_sem, recv_sem, {axis: to})
        pending.append((None, dst.at[pl.ds(0, 15)], send_sem))

    def finished(ref, sem):
        pltpu.make_async_copy(ref, ref, sem).wait()

    def await_all(dst, sem):
        finished(dst.at[pl.ds(0, 15)], sem)

    coarse8[...] = jnp.zeros_like(coarse8)
    loads[1].wait()
    coarse8[0, 0:6, :] = coarse_ref[:, 0, :]
    row_i = lax.broadcasted_iota(jnp.int32, (96, 128), 0)
    lane_i = lax.broadcasted_iota(jnp.int32, (96, 128), 1)
    spread = ((row_i == (lane_i >> 3) * 6 + (lane_i & 7)) & ((lane_i & 7) < 6)).astype(f32)
    row_8 = lax.broadcasted_iota(jnp.int32, (8, 128), 0)
    lane_8 = lax.broadcasted_iota(jnp.int32, (8, 128), 1)
    lane_blk = lane_8 >> 3
    passing = ((row_8 >= 6) & ((lane_8 & 7) == row_8)).astype(f32)
    for r in range(NR):
        piece = coarse8[0, :, 96 * r:96 * r + 96]
        wide = jnp.dot(piece, spread, preferred_element_type=f32, precision=lax.Precision.HIGHEST)
        wide = wide + passing
        kown[r] = wide

    for ref in al_all:
        ref[4] = jnp.zeros((8, NRHS), f32)
    for ref in al_near:
        ref[2] = jnp.zeros((8, NRHS), f32)
    corr[2] = jnp.zeros((FACE, NRHS), f32)
    for ref in face_in:
        ref[4] = jnp.zeros((FACE, NRHS), f32)
    for f in range(4):
        @pl.when(jnp.logical_not(present[f]))
        def _(f=f):
            if f < 2:
                t_in[f] = jnp.zeros((8, 128), f32)
            for ref in al_all:
                ref[f] = jnp.zeros((8, NRHS), f32)
            if f >= 2:
                for ref in al_near:
                    ref[f - 2] = jnp.zeros((8, NRHS), f32)
            for ref in face_in:
                ref[f] = jnp.zeros((FACE, NRHS), f32)

    loads[2].wait()
    loads[3].wait()
    for i in range(NL // 128):
        signs = glue_ref[0:1, 128 * i:128 * i + 128].astype(f32)
        glue_b[128 * i:128 * i + 128, :] = jnp.broadcast_to(signs, (128, 128)).T
        plain = jnp.concatenate(
            [modes_ref[:, 0, 128 * i:128 * i + 128], jnp.zeros((2, 128), f32)], axis=0
        )
        hi = plain.astype(bf16).astype(f32)
        u16[:, 128 * i:128 * i + 128] = jnp.concatenate([hi, plain - hi], axis=0).astype(bf16)
        signed = plain * signs
        hi = signed.astype(bf16).astype(f32)
        m16[:, 128 * i:128 * i + 128] = jnp.concatenate([hi, signed - hi], axis=0).astype(bf16)
        stacked = jnp.concatenate(
            [hi, hi, signed - hi, jnp.zeros((104, 128), f32)], axis=0
        ).T
        half = 128 * (i % 2)
        mt[i // 2, half:half + 128, :] = stacked[:, 0:32].astype(bf16)

    facing = []
    across = []
    beside = []
    share = []
    for j in range(SLOTS):
        where = jnp.int32(4)
        weight = jnp.float32(1.0)
        for f in range(4):
            hit = slot_ref[0, f] == j
            where = jnp.where(hit, f, where)
            weight = jnp.where(jnp.logical_and(hit, present[f]), 0.5, weight)
        facing.append(where)
        across.append(jnp.where(where < 2, where, 2))
        beside.append(jnp.where(jnp.logical_and(where >= 2, where < 4), where - 2, 2))
        share.append(weight)

    def swap_amplitudes(k, others):
        for f in others:
            @pl.when(present[f])
            def _(f=f):
                send(
                    a_out.at[k], al_all[k].at[f ^ 1], a_send.at[k, f], a_recv.at[k, f ^ 1], peer[f]
                )

            pending.append((present[f], a_out.at[k], a_send.at[k, f]))

    def amplitude_done(k, others):
        for f in others:
            @pl.when(present[f])
            def _(f=f):
                pltpu.make_async_copy(a_out.at[k], al_all[k].at[f], a_recv.at[k, f]).wait()

    def spread_modes(modes, q):
        hi = q.astype(bf16).astype(f32)
        stacked = jnp.concatenate([hi, q - hi, hi, jnp.zeros_like(q)], axis=0).astype(bf16)
        return dot(modes, stacked)

    def product(matrix, j):
        rows = slice(FACE * j, FACE * j + FACE)
        return glue_b[rows, :] * dot(matrix[rows, :], low[...])

    def lower(j, value):
        rows = slice(FACE * j, FACE * j + FACE)
        low[rows, :] = (glue_b[rows, :] * value).astype(bf16)

    def add_up(part):
        return part[:8] + part[8:]

    def sums_of(matrix, target, weights):
        for j in range(SLOTS):
            rows = slice(FACE * j, FACE * j + FACE)
            wide = add_up(dot(u16[:, rows], matrix[rows, :])) * weights[j]
            hi = wide.astype(bf16).astype(f32)
            target[16 * j:16 * j + 16, :] = jnp.concatenate([hi, wide - hi], axis=0).astype(bf16)

    def hand_out(mine, all_of, send_sem, recv_sem):
        for p in (8, 6, 10, 4, 12, 2, 14):
            to = {"block": lax.rem(block + p, NBK)}
            send(mine, all_of.at[block], send_sem.at[0], recv_sem.at[0], to)
        send(mine, all_of.at[block], send_sem.at[0], recv_sem.at[0], sibling)
        pending.append((None, all_of.at[pl.ds(0, 8)], send_sem.at[0]))

    def hand_on(all_of, send_sem, recv_sem):
        finished(all_of.at[pl.ds(0, 8)], recv_sem.at[0])
        for p in range(2, 16, 2):
            at = lax.rem(block + p, NBK)
            send(all_of.at[at], all_of.at[at], send_sem.at[1], recv_sem.at[1], sibling)
        pending.append((None, all_of.at[pl.ds(0, 7)], send_sem.at[1]))

    def coupling():
        plain = u16[0:8, :].astype(f32) + u16[8:16, :].astype(f32)
        slot_at = lax.broadcasted_iota(jnp.int32, (8, NL), 1) >> 8
        groups = [plain]
        for f in range(4):
            weight = jnp.where(present[f], -1.0, 0.0)
            groups.append(jnp.where(slot_at == slot_ref[0, f], plain, 0.0) * weight)
        stack = jnp.concatenate(groups + [jnp.zeros((8, NL), f32)], axis=0)
        hi = stack.astype(bf16).astype(f32)
        lo = stack - hi
        wide = dot(jnp.concatenate([hi, lo], axis=0).astype(bf16), dmat[...])
        w_hi, w_lo = split(wide[:48] + wide[48:])
        fill = jnp.zeros((80, NL), f32)
        v_hi = jnp.concatenate([hi, fill], axis=0).astype(bf16)
        v_lo = jnp.concatenate([lo, fill], axis=0).astype(bf16)

        def across_rows(a, b):
            return lax.dot_general(a, b, (((1,), (1,)), ((), ())), preferred_element_type=f32)

        square = across_rows(w_hi, v_hi) + across_rows(w_lo, v_hi) + across_rows(w_hi, v_lo)
        ybuf[...] = jnp.zeros_like(ybuf)
        ybuf[rows8(block), :] = square[0:8]
        for f in range(4):
            @pl.when(present[f])
            def _(f=f):
                ybuf[rows8(place[f]), :] = square[8 * f + 8:8 * f + 16]
        turned = ybuf[...].T
        for g in range(5):
            lown[g] = turned[8 * g:8 * g + 8, :]

    def coupling_send():
        hand_out(lown, ldist, ld_send, ld_recv)
        ldist[block] = lown[...]

    loads[4].wait()
    for j in range(SLOTS):
        rows = slice(FACE * j, FACE * j + FACE)
        hi, lo = split(gap_v[rows, :])
        gcoef[j] = add_up(dot(m16[:, rows], hi) + dot(m16[:, rows], lo))

    own_rows = pl.ds(block * 6, 6)
    loads[0].wait()
    pl.semaphore_wait(barrier, 30)
    for p in FAR_FIRST:
        send(
            loads_ref, g1_in.at[own_rows], st_send.at[0, 0], st_recv.at[0, 0],
            {"block": lax.rem(block + p, NBK)},
        )
    pending.append((None, g1_in.at[pl.ds(0, 90)], st_send.at[0, 0]))
    send(coarse_ref, coarse_sib, sib_send.at[0], sib_recv.at[0], sibling)
    pending.append((None, coarse_sib, sib_send.at[0]))
    g1_in[own_rows] = loads_ref[...]

    loads[5].wait()
    sums_of(dmat, dcoef, [1.0] * SLOTS)
    finished(coarse_sib, sib_recv.at[0])
    coarse8[1, 0:6, :] = coarse_sib[:, 0, :]
    for r in range(NR):
        pieces = []
        for c in range(2):
            piece = coarse8[c, :, 96 * r:96 * r + 96]
            hi = piece.astype(bf16).astype(f32)
            pieces += [hi, piece - hi]
        kpair[r] = jnp.concatenate(pieces, axis=0).astype(bf16)

    finished(g1_in.at[pl.ds(0, 90)], st_recv.at[0, 0])
    for i in (4, 3, 5, 2, 6, 1, 7):
        to = lax.rem(region + 2 * i + core, NR)
        send(
            g1_in, g1_all.at[region], st_send.at[0, 1], st_recv.at[0, 1], {"region": to}
        )

    @pl.when(core == 1)
    def _():
        send(
            g1_in, g1_all.at[region], st_send.at[0, 1], st_recv.at[0, 1],
            {"region": lax.rem(region + 1, NR)},
        )

    pending.append((core == 0, g1_all.at[pl.ds(0, 7)], st_send.at[0, 1]))
    pending.append((core == 1, g1_all.at[pl.ds(0, 8)], st_send.at[0, 1]))

    @pl.when(core == 0)
    def _():
        g1_all[region] = g1_in[...]

    hand_out(kown, kdist, kd_send, kd_recv)
    kdist[block] = kown[...]

    loads[6].wait()
    sums_of(emat, ecoef, share)
    coupling()

    for c, count in ((0, 7), (1, 8)):
        @pl.when(core == c)
        def _(count=count):
            finished(g1_all.at[pl.ds(0, count)], st_recv.at[0, 1])

    total = jnp.zeros((32, NRHS), f32)
    for i in range(8):
        at = 2 * i + lax.rem(region + core, 2)
        hi, lo = split(g1_all[at, :, 0, :])
        total = total + (dot(kpair[at], hi) + dot(kpair[at], lo))
    half_out[...] = add_up(total[16:])
    send(half_out, half_in, sib_send.at[1], sib_recv.at[1], sibling)
    pending.append((None, half_out, sib_send.at[1]))
    finished(half_in, sib_recv.at[1])
    a_out[0] = add_up(total[:16]) + half_in[...]
    swap_amplitudes(0, range(4))
    xbuf[...] = jnp.zeros_like(xbuf)
    amplitude_done(0, range(4))
    for j in range(SLOTS):
        value = spread_modes(mt[j], a_out[0] - al_all[0][facing[j]])
        lam[j] = value
        lower(j, value)

    def sum_start(out, arrived, k, stage):
        axis, me = (("block", block), ("region", region))[stage]
        all_to(
            axis, me, lambda to: out.at[stage], arrived.at[stage],
            st_send.at[k, stage], st_recv.at[k, stage],
        )
        arrived[stage, me] = out[stage]

    def sum_wait(out, arrived, k, stage):
        await_all(arrived.at[stage], st_recv.at[k, stage])
        out[stage + 1] = jnp.sum(arrived[stage], axis=0)

    def send_faces(k):
        for f in range(4):
            @pl.when(present[f])
            def _(f=f):
                send(
                    face_out.at[k - 1, f], face_in[k - 1].at[f ^ 1],
                    fc_send.at[k - 1, f], fc_recv.at[k - 1, f ^ 1], peer[f],
                )

            pending.append((present[f], face_out.at[k - 1, f], fc_send.at[k - 1, f]))

    def gather_send(k, coef, sign):
        both = dot(coef[...], low[...])
        mine = None
        for j in range(SLOTS):
            term = add_up(both[16 * j:16 * j + 16])
            if sign < 0:
                term = gcoef[j] - term
            pbuf[j] = term
            mine = term if mine is None else mine + term
        xbuf[rows8(block), :] = mine
        for f in range(4):
            term = pbuf[slot_ref[0, f]]

            @pl.when(present[f])
            def _(f=f, term=term):
                xbuf[rows8(place[f]), :] = -term
        s1_out[k] = xbuf[...].T.reshape(16, 8, 128)
        all_to(
            "block", block, lambda to: s1_out.at[k, to], s1_in.at[k],
            st_send.at[k, 0], st_recv.at[k, 0],
        )
        s1_in[k, block] = s1_out[k, block]

    def faces_send(k):
        for f in range(4):
            face_out[k - 1, f] = wloc[slot_ref[0, f]]
        send_faces(k)

    def gathered(k):
        await_all(s1_in.at[k], st_recv.at[k, 0])
        main = jnp.zeros((8, 128), f32)
        before = jnp.zeros((8, 128), f32)
        after = jnp.zeros((8, 128), f32)
        for t in range(NBK):
            tile = s1_in[k, t]
            main = main + jnp.where((lane_blk >= t - 1) & (lane_blk <= t + 1), tile, 0.0)
            before = before + jnp.where(lane_blk == (t + 8) % 16, tile, 0.0)
            after = after + jnp.where(lane_blk == (t + 9) % 16, tile, 0.0)
        return main, pltpu.roll(before, 64, 1), pltpu.roll(after, 56, 1)

    def regions_send(k, tiles):
        for i in range(3):
            s2_out[k, i] = tiles[i]
        all_to(
            "region", region, lambda to: s2_out.at[k], s2_in.at[k],
            st_send.at[k, 1], st_recv.at[k, 1],
        )
        s2_in[k, region] = s2_out[k]

    def solved(k):
        await_all(s2_in.at[k], st_recv.at[k, 1])
        pieces = []
        for r in range(NR):
            tile = s2_in[k, r, 0]
            if r < NR - 1:
                tile = tile + s2_in[k, r + 1, 1]
            if r > 0:
                tile = tile + s2_in[k, r - 1, 2]
            hi = tile.astype(bf16).astype(f32)
            pieces.append(jnp.concatenate([hi, tile - hi], axis=0).astype(bf16))
        left = jnp.concatenate(pieces, axis=1)
        both = dot(left, khi[...]) + dot(left, klo[...])
        s3_out[k] = both[:8] + both[8:]
        all_to(
            "block", block, lambda to: s3_out.at[k], s3_in.at[k],
            st_send.at[k, 2], st_recv.at[k, 2],
        )
        s3_in[k, block] = s3_out[k]

    def returned(k):
        await_all(s3_in.at[k], st_recv.at[k, 2])
        abuf[...] = s3_in[k].reshape(128, 128).T
        a_out[k] = abuf[rows8(block), :]
        swap_amplitudes(k, range(2))
        for f, near in ((2, block - 1), (3, block + 1)):
            @pl.when(present[f])
            def _(f=f, near=near):
                al_near[k][f - 2] = abuf[rows8(near), :]

    def faces_wait(k):
        for f in range(4):
            @pl.when(present[f])
            def _(f=f):
                pltpu.make_async_copy(
                    face_out.at[k - 1, f], face_in[k - 1].at[f], fc_recv.at[k - 1, f]
                ).wait()

    def whole(k, j):
        return wloc[j] + face_in[k - 1][facing[j]]

    def less_field(k, value_of):
        for j in range(SLOTS):
            near = spread_modes(mt[j], a_out[k] - al_near[k][beside[j]])
            part[j] = value_of(j) - near
        amplitude_done(k, range(2))
        for f in range(2):
            corr[f] = spread_modes(mt[slot_ref[0, f]], al_all[k][f])

    def assembled(j):
        return part[j] + corr[across[j]]

    def coarse_round(k, coef, sign, multiply, prepare):
        gather_send(k, coef, sign)
        multiply()
        faces_send(k)
        regions_send(k, gathered(k))
        prepare()
        solved(k)
        returned(k)
        faces_wait(k)
        less_field(k, lambda j: whole(k, j))

    def inner(total, left, right):
        return total + jnp.sum((left * right).reshape(FACE // 8, 8, NRHS), axis=0)

    def finish(total):
        return jnp.sum(total, axis=0, keepdims=True)

    zero8 = jnp.zeros((8, NRHS), f32)

    def coarse_matrix():
        finished(kdist.at[pl.ds(0, 7)], kd_recv.at[1])
        for r in range(NR):
            hi, lo = split(kdist[:, r].reshape(128, 128).T)
            khi[128 * r:128 * r + 128, :] = hi
            klo[128 * r:128 * r + 128, :] = lo

    def dual_start():
        for j in range(SLOTS):
            wloc[j] = gap_v[FACE * j:FACE * j + FACE, :] - product(dmat, j)
        hand_on(kdist, kd_send, kd_recv)

    def dirichlet():
        for j in range(SLOTS):
            wloc[j] = share[j] * product(emat, j)

    def unpacked(tile, b):
        before = jnp.where(lane_blk == (b + 8) % 16, tile, 0.0)
        after = jnp.where(lane_blk == (b + 9) % 16, tile, 0.0)
        return (
            jnp.where((lane_blk >= b - 1) & (lane_blk <= b + 1), tile, 0.0),
            pltpu.roll(before, 64, 1), pltpu.roll(after, 56, 1),
        )

    def coupling_matrix():
        finished(ldist.at[pl.ds(0, 7)], ld_recv.at[1])
        lmat[...] = jnp.zeros_like(lmat)
        for b in range(NBK):
            for g, at in enumerate((b + 16, b, b + 32, b + 15, b + 17)):
                if (g == 3 and b == 0) or (g == 4 and b == NBK - 1):
                    continue
                rows = slice(8 * at, 8 * at + 8)
                tile = ldist[b, g]
                for c, column in zip((128, 0, 256), unpacked(tile, b)):
                    lmat[rows, c:c + 128] = lmat[rows, c:c + 128] + column
        hi, lo = split(lmat[...])
        lhi[...] = hi
        llo[...] = lo

    def prepared():
        coupling_send()
        coarse_matrix()

    coarse_round(1, dcoef, -1, dual_start, prepared)
    for j in range(SLOTS):
        value = assembled(j)
        search[j] = value
        lower(j, share[j] * value)

    gather_send(2, ecoef, 1)
    dirichlet()
    faces_send(2)
    regions_send(2, gathered(2))
    faces_wait(2)
    for j in range(SLOTS):
        value = whole(2, j)
        direc[j] = value
        lower(j, value)
    gather_send(3, dcoef, 1)
    hand_on(ldist, ld_send, ld_recv)
    solved(2)
    for f in range(2):
        @pl.when(present[f])
        def _(f=f):
            send(s3_out.at[2], t_in.at[f ^ 1], t_send.at[f], t_recv.at[f ^ 1], peer[f])

        pending.append((present[f], s3_out.at[2], t_send.at[f]))
    coupling_matrix()
    tiles = gathered(3)
    for f in range(2):
        @pl.when(present[f])
        def _(f=f):
            finished(t_in.at[f], t_recv.at[f])
    pieces = []
    for tile in (t_in[0], s3_out[2], t_in[1]):
        hi = tile.astype(bf16).astype(f32)
        pieces.append(jnp.concatenate([hi, tile - hi], axis=0).astype(bf16))
    left = jnp.concatenate(pieces, axis=1)
    coupled = add_up(dot(left, lhi[...]) + dot(left, llo[...]))
    regions_send(
        3,
        (tiles[0] - coupled[:, 128:256], tiles[1] - coupled[:, 0:128], tiles[2] - coupled[:, 256:]),
    )
    returned(2)
    less_field(2, lambda j: direc[j])
    energy = zero8
    for j in range(SLOTS):
        value = assembled(j)
        direc[j] = value
        lower(j, value)
        energy = inner(energy, share[j] * search[j], value)
    curvature = zero8
    for j in range(SLOTS):
        value = product(dmat, j)
        wloc[j] = value
        field[j] = value
        curvature = inner(curvature, direc[j], value)
    c_out[0] = jnp.concatenate(
        [finish(energy), finish(curvature), jnp.zeros((6, NRHS), f32)], axis=0
    )
    sum_start(c_out, c_in, 6, 0)
    faces_send(3)
    solved(3)
    sum_wait(c_out, c_in, 6, 0)
    sum_start(c_out, c_in, 6, 1)
    returned(3)
    faces_wait(3)
    less_field(3, lambda j: whole(3, j))
    sum_wait(c_out, c_in, 6, 1)
    energy0 = c_out[2, 0:1, :]
    curvature0 = c_out[2, 1:2, :]
    step0 = energy0 / curvature0

    for j in range(SLOTS):
        value = search[j] - step0 * assembled(j)
        search[j] = value
        lower(j, share[j] * value)

    coarse_round(4, ecoef, 1, dirichlet, lambda: None)
    energy = zero8
    cross = zero8
    for j in range(SLOTS):
        value = assembled(j)
        lower(j, value)
        energy = inner(energy, share[j] * search[j], value)
        cross = inner(cross, value, field[j])
        search[j] = value
    curvature = zero8
    for j in range(SLOTS):
        curvature = inner(curvature, search[j], product(dmat, j))
    f_out[0] = jnp.concatenate(
        [finish(energy), finish(curvature), finish(cross), jnp.zeros((5, NRHS), f32)], axis=0
    )
    for stage in range(2):
        sum_start(f_out, f_in, 5, stage)
        sum_wait(f_out, f_in, 5, stage)
    energy1 = f_out[2, 0:1, :]
    beta = energy1 / energy0
    curvature1 = f_out[2, 1:2, :] + 2.0 * beta * f_out[2, 2:3, :] + beta * beta * curvature0
    step1 = energy1 / curvature1
    first = step0 + step1 * beta
    for j in range(SLOTS):
        out_ref[FACE * j:FACE * j + FACE, :] = lam[j] + first * direc[j] + step1 * search[j]

    for condition, ref, sem in pending:
        if condition is None:
            finished(ref, sem)
        else:
            @pl.when(condition)
            def _(ref=ref, sem=sem):
                finished(ref, sem)


def body(
    gap_terms, rigid_loads, dual_matrix, dirichlet_matrix, rigid_modes, coarse_rows,
    face_slot, glue_sign,
):
    vmem = pl.BlockSpec(memory_space=pltpu.VMEM)
    hbm = pl.BlockSpec(memory_space=pl.ANY)
    V = pltpu.VMEM
    slots = (SLOTS, FACE, NRHS)
    scratch = [
        V((6, 1, NRHS), f32), V((6, 1, NL), f32), V((6, 1, NL), f32), V((1, NL), jnp.int32),
        V((NL, NL), bf16), V((NL, NL), bf16), V((NL, NRHS), f32), V((NL, NRHS), f32),
        V((16, NL), bf16), V((16, NL), bf16), V((SLOTS, FACE, 32), bf16), V((2, 8, NL), f32),
        V((6, 1, NL), f32), V((NR, 32, 96), bf16), V((NR, 8, 128), f32), V((NBK, NR, 8, 128), f32),
        V((NR * 128, 128), bf16), V((NR * 128, 128), bf16),
        V((96, NL), bf16), V((96, NL), bf16), V((SLOTS, 8, NRHS), f32),
        V((128, 128), f32), V((5, 8, 128), f32), V((NBK, 5, 8, 128), f32),
        V((384, 384), f32), V((384, 384), bf16), V((384, 384), bf16), V((2, 8, 128), f32),
        V(slots, f32), V(slots, f32), V(slots, f32), V(slots, f32), V(slots, f32),
        V((NL, NRHS), bf16), V((SLOTS, 8, NRHS), f32), V((128, 128), f32), V((128, 128), f32),
        V((96, 1, 128), f32), V((NR, 96, 1, 128), f32), V((8, 128), f32), V((8, 128), f32),
        V((ROUNDS, NBK, 8, 128), f32), V((ROUNDS, NBK, 8, 128), f32),
        V((ROUNDS, 3, 8, 128), f32), V((ROUNDS, NR, 3, 8, 128), f32),
        V((ROUNDS, 8, 128), f32), V((ROUNDS, NBK, 8, 128), f32),
        V((ROUNDS, 8, 128), f32), tuple(V((5, 8, 128), f32) for _ in range(ROUNDS)),
        tuple(V((3, 8, 128), f32) for _ in range(ROUNDS)), V(slots, f32), V((3, FACE, NRHS), f32),
        V((4, 4, FACE, NRHS), f32), tuple(V((5, FACE, NRHS), f32) for _ in range(4)),
        V((3, 8, 128), f32), V((2, 16, 8, 128), f32),
        V((3, 8, 128), f32), V((2, 16, 8, 128), f32),
        pltpu.SemaphoreType.DMA((7,)), pltpu.SemaphoreType.DMA((2,)), pltpu.SemaphoreType.DMA((2,)),
        pltpu.SemaphoreType.DMA((2,)), pltpu.SemaphoreType.DMA((2,)),
        pltpu.SemaphoreType.DMA((2,)), pltpu.SemaphoreType.DMA((2,)),
        pltpu.SemaphoreType.DMA((2,)), pltpu.SemaphoreType.DMA((2,)),
        pltpu.SemaphoreType.DMA((ROUNDS + 2, 3)), pltpu.SemaphoreType.DMA((ROUNDS + 2, 3)),
        pltpu.SemaphoreType.DMA((ROUNDS, 4)), pltpu.SemaphoreType.DMA((ROUNDS, 4)),
        pltpu.SemaphoreType.DMA((4, 4)), pltpu.SemaphoreType.DMA((4, 4)),
    ]
    result = pl.pallas_call(
        kernel,
        out_shape=jax.ShapeDtypeStruct((NL, NRHS), f32),
        in_specs=[hbm] * 6 + [pl.BlockSpec(memory_space=pltpu.SMEM), hbm],
        out_specs=vmem,
        scratch_shapes=scratch,
        compiler_params=pltpu.CompilerParams(
            collective_id=0, has_side_effects=True, vmem_limit_bytes=60 * 1024 * 1024,
        ),
        cost_estimate=pl.CostEstimate(
            flops=5 * 2 * NL * NL * NRHS, bytes_accessed=12 * 1024 * 1024, transcendentals=0
        ),
    )(
        gap_terms, rigid_loads.transpose(0, 2, 1, 3), dual_matrix, dirichlet_matrix,
        rigid_modes.transpose(0, 2, 1, 3), coarse_rows.transpose(0, 2, 1, 3),
        face_slot, glue_sign,
    )
    return result[None, None]


def solution(mesh):
    matrix = P("region", "block", None, None)
    vector = P("region", "block", None)
    return jax.shard_map(
        body, mesh=mesh, in_specs=(matrix,) * 6 + (vector,) * 2, out_specs=matrix,
        check_vma=False,
    )
```

```python
import jax
import jax.numpy as jnp
from jax import lax
from jax.experimental import pallas as pl
from jax.experimental.pallas import tpu as pltpu
from jax.sharding import PartitionSpec as P

FACE = 256
SLOTS = 6
NL = FACE * SLOTS
NRHS = 128
NR = 16
NBK = 16
FAR_FIRST = (8, 7, 9, 6, 10, 5, 11, 4, 12, 3, 13, 2, 14, 1, 15)
ROUNDS = 5

f32 = jnp.float32
bf16 = jnp.bfloat16
MESH = pl.DeviceIdType.MESH


def split(x):
    hi = x.astype(bf16)
    lo = (x - hi.astype(f32)).astype(bf16)
    return hi, lo


def dot(a, b):
    return jnp.dot(a, b, preferred_element_type=f32)


def kernel(
    gap_hbm, loads_hbm, dual_hbm, diri_hbm, modes_hbm, coarse_hbm, slot_arg, glue_hbm,
    out_ref,
    loads_ref, modes_ref, coarse_ref, glue_ref,
    dmat, emat, gap_v, glue_b, m16, u16, mt, coarse8, coarse_sib, kpair, kown, kdist, khi, klo,
    dcoef, ecoef, gcoef, ybuf, lown, ldist, lmat, lhi, llo, t_in,
    lam, search, direc, wloc, field, low, pbuf, xbuf, abuf,
    g1_in, g1_all, half_out, half_in, s1_out, s1_in, s2_out, s2_in, s3_out, s3_in,
    a_out, al_all, al_near, part, corr, face_out, face_in, f_out, f_in, c_out, c_in,
    load_sem, kd_send, kd_recv, ld_send, ld_recv, t_send, t_recv, sib_send, sib_recv, st_send, st_recv, a_send, a_recv, fc_send, fc_recv,
):
    region = lax.axis_index("region")
    block = lax.axis_index("block")
    present = [region > 0, region < NR - 1, block > 0, block < NBK - 1]
    peer = [
        {"region": region - 1}, {"region": region + 1},
        {"block": block - 1}, {"block": block + 1},
    ]

    def rows8(index):
        return pl.ds(pl.multiple_of(index * 8, 8), 8)

    slot_ref = slot_arg.at[0]
    core = lax.rem(block, 2)
    place = [lax.rem(block + 8, 16), lax.rem(block + 9, 16), block - 1, block + 1]
    sibling = {"block": block + 1 - 2 * core}
    barrier = pltpu.get_barrier_semaphore()
    for p in range(1, 16):
        pl.semaphore_signal(
            barrier, inc=1, device_id={"block": lax.rem(block + p, NBK)}, device_id_type=MESH
        )
        pl.semaphore_signal(
            barrier, inc=1, device_id={"region": lax.rem(region + p, NR)}, device_id_type=MESH
        )

    loads = [
        pltpu.make_async_copy(source, target, load_sem.at[i])
        for i, (source, target) in enumerate((
            (loads_hbm.at[0], loads_ref), (coarse_hbm.at[0], coarse_ref),
            (glue_hbm.at[0], glue_ref), (modes_hbm.at[0], modes_ref),
            (gap_hbm.at[0, 0], gap_v), (dual_hbm.at[0, 0], dmat), (diri_hbm.at[0, 0], emat),
        ))
    ]
    for copy in loads:
        copy.start()

    pending = []

    def send(src, dst, send_sem, recv_sem, target):
        pltpu.make_async_remote_copy(
            src_ref=src, dst_ref=dst, send_sem=send_sem, recv_sem=recv_sem,
            device_id=target, device_id_type=MESH,
        ).start()

    def all_to(axis, me, src, dst, send_sem, recv_sem):
        for p in FAR_FIRST:
            to = lax.rem(me + p, 16)
            send(src(to), dst.at[me], send_sem, recv_sem, {axis: to})
        pending.append((None, dst.at[pl.ds(0, 15)], send_sem))

    def finished(ref, sem):
        pltpu.make_async_copy(ref, ref, sem).wait()

    def await_all(dst, sem):
        finished(dst.at[pl.ds(0, 15)], sem)

    coarse8[...] = jnp.zeros_like(coarse8)
    loads[1].wait()
    coarse8[0, 0:6, :] = coarse_ref[:, 0, :]
    row_i = lax.broadcasted_iota(jnp.int32, (96, 128), 0)
    lane_i = lax.broadcasted_iota(jnp.int32, (96, 128), 1)
    spread = ((row_i == (lane_i >> 3) * 6 + (lane_i & 7)) & ((lane_i & 7) < 6)).astype(f32)
    row_8 = lax.broadcasted_iota(jnp.int32, (8, 128), 0)
    lane_8 = lax.broadcasted_iota(jnp.int32, (8, 128), 1)
    lane_blk = lane_8 >> 3
    passing = ((row_8 >= 6) & ((lane_8 & 7) == row_8)).astype(f32)
    for r in range(NR):
        piece = coarse8[0, :, 96 * r:96 * r + 96]
        wide = jnp.dot(piece, spread, preferred_element_type=f32, precision=lax.Precision.HIGHEST)
        wide = wide + passing
        kown[r] = wide

    for ref in al_all:
        ref[4] = jnp.zeros((8, NRHS), f32)
    for ref in al_near:
        ref[2] = jnp.zeros((8, NRHS), f32)
    corr[2] = jnp.zeros((FACE, NRHS), f32)
    for ref in face_in:
        ref[4] = jnp.zeros((FACE, NRHS), f32)
    for f in range(4):
        @pl.when(jnp.logical_not(present[f]))
        def _(f=f):
            if f < 2:
                for ref in t_in:
                    ref[f] = jnp.zeros((8, 128), f32)
            for ref in al_all:
                ref[f] = jnp.zeros((8, NRHS), f32)
            if f >= 2:
                for ref in al_near:
                    ref[f - 2] = jnp.zeros((8, NRHS), f32)
            for ref in face_in:
                ref[f] = jnp.zeros((FACE, NRHS), f32)

    loads[2].wait()
    loads[3].wait()
    for i in range(NL // 128):
        signs = glue_ref[0:1, 128 * i:128 * i + 128].astype(f32)
        glue_b[128 * i:128 * i + 128, :] = jnp.broadcast_to(signs, (128, 128)).T
        plain = jnp.concatenate(
            [modes_ref[:, 0, 128 * i:128 * i + 128], jnp.zeros((2, 128), f32)], axis=0
        )
        hi = plain.astype(bf16).astype(f32)
        u16[:, 128 * i:128 * i + 128] = jnp.concatenate([hi, plain - hi], axis=0).astype(bf16)
        signed = plain * signs
        hi = signed.astype(bf16).astype(f32)
        m16[:, 128 * i:128 * i + 128] = jnp.concatenate([hi, signed - hi], axis=0).astype(bf16)
        stacked = jnp.concatenate(
            [hi, hi, signed - hi, jnp.zeros((104, 128), f32)], axis=0
        ).T
        half = 128 * (i % 2)
        mt[i // 2, half:half + 128, :] = stacked[:, 0:32].astype(bf16)

    facing = []
    across = []
    beside = []
    share = []
    for j in range(SLOTS):
        where = jnp.int32(4)
        weight = jnp.float32(1.0)
        for f in range(4):
            hit = slot_ref[0, f] == j
            where = jnp.where(hit, f, where)
            weight = jnp.where(jnp.logical_and(hit, present[f]), 0.5, weight)
        facing.append(where)
        across.append(jnp.where(where < 2, where, 2))
        beside.append(jnp.where(jnp.logical_and(where >= 2, where < 4), where - 2, 2))
        share.append(weight)

    def swap_amplitudes(k, others):
        for f in others:
            @pl.when(present[f])
            def _(f=f):
                send(
                    a_out.at[k], al_all[k].at[f ^ 1], a_send.at[k, f], a_recv.at[k, f ^ 1], peer[f]
                )

            pending.append((present[f], a_out.at[k], a_send.at[k, f]))

    def amplitude_done(k, others):
        for f in others:
            @pl.when(present[f])
            def _(f=f):
                pltpu.make_async_copy(a_out.at[k], al_all[k].at[f], a_recv.at[k, f]).wait()

    def spread_modes(modes, q):
        hi = q.astype(bf16).astype(f32)
        stacked = jnp.concatenate([hi, q - hi, hi, jnp.zeros_like(q)], axis=0).astype(bf16)
        return dot(modes, stacked)

    def product(matrix, j):
        rows = slice(FACE * j, FACE * j + FACE)
        return glue_b[rows, :] * dot(matrix[rows, :], low[...])

    def lower(j, value):
        rows = slice(FACE * j, FACE * j + FACE)
        low[rows, :] = (glue_b[rows, :] * value).astype(bf16)

    def add_up(part):
        return part[:8] + part[8:]

    def sums_of(matrix, target, weights):
        for j in range(SLOTS):
            rows = slice(FACE * j, FACE * j + FACE)
            wide = add_up(dot(u16[:, rows], matrix[rows, :])) * weights[j]
            hi = wide.astype(bf16).astype(f32)
            target[16 * j:16 * j + 16, :] = jnp.concatenate([hi, wide - hi], axis=0).astype(bf16)

    def hand_out(mine, all_of, send_sem, recv_sem):
        for p in (8, 6, 10, 4, 12, 2, 14):
            to = {"block": lax.rem(block + p, NBK)}
            send(mine, all_of.at[block], send_sem.at[0], recv_sem.at[0], to)
        send(mine, all_of.at[block], send_sem.at[0], recv_sem.at[0], sibling)
        pending.append((None, all_of.at[pl.ds(0, 8)], send_sem.at[0]))

    def hand_on(all_of, send_sem, recv_sem):
        finished(all_of.at[pl.ds(0, 8)], recv_sem.at[0])
        for p in range(2, 16, 2):
            at = lax.rem(block + p, NBK)
            send(all_of.at[at], all_of.at[at], send_sem.at[1], recv_sem.at[1], sibling)
        pending.append((None, all_of.at[pl.ds(0, 7)], send_sem.at[1]))

    def coupling():
        plain = u16[0:8, :].astype(f32) + u16[8:16, :].astype(f32)
        slot_at = lax.broadcasted_iota(jnp.int32, (8, NL), 1) >> 8
        groups = [plain]
        for f in range(4):
            weight = jnp.where(present[f], -1.0, 0.0)
            groups.append(jnp.where(slot_at == slot_ref[0, f], plain, 0.0) * weight)
        stack = jnp.concatenate(groups + [jnp.zeros((8, NL), f32)], axis=0)
        hi = stack.astype(bf16).astype(f32)
        lo = stack - hi
        wide = dot(jnp.concatenate([hi, lo], axis=0).astype(bf16), dmat[...])
        w_hi, w_lo = split(wide[:48] + wide[48:])
        fill = jnp.zeros((80, NL), f32)
        v_hi = jnp.concatenate([hi, fill], axis=0).astype(bf16)
        v_lo = jnp.concatenate([lo, fill], axis=0).astype(bf16)

        def across_rows(a, b):
            return lax.dot_general(a, b, (((1,), (1,)), ((), ())), preferred_element_type=f32)

        square = across_rows(w_hi, v_hi) + across_rows(w_lo, v_hi) + across_rows(w_hi, v_lo)
        ybuf[...] = jnp.zeros_like(ybuf)
        ybuf[rows8(block), :] = square[0:8]
        for f in range(4):
            @pl.when(present[f])
            def _(f=f):
                ybuf[rows8(place[f]), :] = square[8 * f + 8:8 * f + 16]
        turned = ybuf[...].T
        for g in range(5):
            lown[g] = turned[8 * g:8 * g + 8, :]

    def coupling_send():
        hand_out(lown, ldist, ld_send, ld_recv)
        ldist[block] = lown[...]

    loads[4].wait()
    for j in range(SLOTS):
        rows = slice(FACE * j, FACE * j + FACE)
        hi, lo = split(gap_v[rows, :])
        gcoef[j] = add_up(dot(m16[:, rows], hi) + dot(m16[:, rows], lo))

    own_rows = pl.ds(block * 6, 6)
    loads[0].wait()
    pl.semaphore_wait(barrier, 30)
    for p in FAR_FIRST:
        send(
            loads_ref, g1_in.at[own_rows], st_send.at[0, 0], st_recv.at[0, 0],
            {"block": lax.rem(block + p, NBK)},
        )
    pending.append((None, g1_in.at[pl.ds(0, 90)], st_send.at[0, 0]))
    send(coarse_ref, coarse_sib, sib_send.at[0], sib_recv.at[0], sibling)
    pending.append((None, coarse_sib, sib_send.at[0]))
    g1_in[own_rows] = loads_ref[...]

    loads[5].wait()
    sums_of(dmat, dcoef, [1.0] * SLOTS)
    finished(coarse_sib, sib_recv.at[0])
    coarse8[1, 0:6, :] = coarse_sib[:, 0, :]
    for r in range(NR):
        pieces = []
        for c in range(2):
            piece = coarse8[c, :, 96 * r:96 * r + 96]
            hi = piece.astype(bf16).astype(f32)
            pieces += [hi, piece - hi]
        kpair[r] = jnp.concatenate(pieces, axis=0).astype(bf16)

    finished(g1_in.at[pl.ds(0, 90)], st_recv.at[0, 0])
    for i in (4, 3, 5, 2, 6, 1, 7):
        to = lax.rem(region + 2 * i + core, NR)
        send(
            g1_in, g1_all.at[region], st_send.at[0, 1], st_recv.at[0, 1], {"region": to}
        )

    @pl.when(core == 1)
    def _():
        send(
            g1_in, g1_all.at[region], st_send.at[0, 1], st_recv.at[0, 1],
            {"region": lax.rem(region + 1, NR)},
        )

    pending.append((core == 0, g1_all.at[pl.ds(0, 7)], st_send.at[0, 1]))
    pending.append((core == 1, g1_all.at[pl.ds(0, 8)], st_send.at[0, 1]))

    @pl.when(core == 0)
    def _():
        g1_all[region] = g1_in[...]

    hand_out(kown, kdist, kd_send, kd_recv)
    kdist[block] = kown[...]

    loads[6].wait()
    sums_of(emat, ecoef, share)
    coupling()

    for c, count in ((0, 7), (1, 8)):
        @pl.when(core == c)
        def _(count=count):
            finished(g1_all.at[pl.ds(0, count)], st_recv.at[0, 1])

    total = jnp.zeros((32, NRHS), f32)
    for i in range(8):
        at = 2 * i + lax.rem(region + core, 2)
        hi, lo = split(g1_all[at, :, 0, :])
        total = total + (dot(kpair[at], hi) + dot(kpair[at], lo))
    half_out[...] = add_up(total[16:])
    send(half_out, half_in, sib_send.at[1], sib_recv.at[1], sibling)
    pending.append((None, half_out, sib_send.at[1]))
    finished(half_in, sib_recv.at[1])
    a_out[0] = add_up(total[:16]) + half_in[...]
    swap_amplitudes(0, range(4))
    xbuf[...] = jnp.zeros_like(xbuf)
    amplitude_done(0, range(4))
    for j in range(SLOTS):
        value = spread_modes(mt[j], a_out[0] - al_all[0][facing[j]])
        lam[j] = value
        lower(j, value)

    def send_faces(k):
        for f in range(4):
            @pl.when(present[f])
            def _(f=f):
                send(
                    face_out.at[k - 1, f], face_in[k - 1].at[f ^ 1],
                    fc_send.at[k - 1, f], fc_recv.at[k - 1, f ^ 1], peer[f],
                )

            pending.append((present[f], face_out.at[k - 1, f], fc_send.at[k - 1, f]))

    def gather_send(k, coef, sign, extra=None, aside=None):
        both = dot(coef[...], low[...])
        mine = extra
        for j in range(SLOTS):
            term = add_up(both[16 * j:16 * j + 16])
            if sign < 0:
                term = gcoef[j] - term
            pbuf[j] = term
            mine = term if mine is None else mine + term
        xbuf[rows8(block), :] = mine
        if aside is not None:
            xbuf[rows8(lax.rem(block + 4, 16)), :] = aside
        for f in range(4):
            term = pbuf[slot_ref[0, f]]

            @pl.when(present[f])
            def _(f=f, term=term):
                xbuf[rows8(place[f]), :] = -term
        s1_out[k] = xbuf[...].T.reshape(16, 8, 128)
        all_to(
            "block", block, lambda to: s1_out.at[k, to], s1_in.at[k],
            st_send.at[k, 0], st_recv.at[k, 0],
        )
        s1_in[k, block] = s1_out[k, block]

    def faces_send(k):
        for f in range(4):
            face_out[k - 1, f] = wloc[slot_ref[0, f]]
        send_faces(k)

    def gathered(k):
        await_all(s1_in.at[k], st_recv.at[k, 0])
        main = jnp.zeros((8, 128), f32)
        before = jnp.zeros((8, 128), f32)
        after = jnp.zeros((8, 128), f32)
        for t in range(NBK):
            tile = s1_in[k, t]
            main = main + jnp.where((lane_blk >= t - 1) & (lane_blk <= t + 1), tile, 0.0)
            before = before + jnp.where(lane_blk == (t + 8) % 16, tile, 0.0)
            after = after + jnp.where(lane_blk == (t + 9) % 16, tile, 0.0)
        return main, pltpu.roll(before, 64, 1), pltpu.roll(after, 56, 1)

    def regions_send(k, tiles):
        for i in range(3):
            s2_out[k, i] = tiles[i]
        all_to(
            "region", region, lambda to: s2_out.at[k], s2_in.at[k],
            st_send.at[k, 1], st_recv.at[k, 1],
        )
        s2_in[k, region] = s2_out[k]

    def solved(k):
        await_all(s2_in.at[k], st_recv.at[k, 1])
        pieces = []
        for r in range(NR):
            tile = s2_in[k, r, 0]
            if r < NR - 1:
                tile = tile + s2_in[k, r + 1, 1]
            if r > 0:
                tile = tile + s2_in[k, r - 1, 2]
            hi = tile.astype(bf16).astype(f32)
            pieces.append(jnp.concatenate([hi, tile - hi], axis=0).astype(bf16))
        left = jnp.concatenate(pieces, axis=1)
        both = dot(left, khi[...]) + dot(left, klo[...])
        s3_out[k] = both[:8] + both[8:]
        all_to(
            "block", block, lambda to: s3_out.at[k], s3_in.at[k],
            st_send.at[k, 2], st_recv.at[k, 2],
        )
        s3_in[k, block] = s3_out[k]

    def returned(k):
        await_all(s3_in.at[k], st_recv.at[k, 2])
        abuf[...] = s3_in[k].reshape(128, 128).T
        a_out[k] = abuf[rows8(block), :]
        swap_amplitudes(k, range(2))
        for f, near in ((2, block - 1), (3, block + 1)):
            @pl.when(present[f])
            def _(f=f, near=near):
                al_near[k][f - 2] = abuf[rows8(near), :]

    def faces_wait(k):
        for f in range(4):
            @pl.when(present[f])
            def _(f=f):
                pltpu.make_async_copy(
                    face_out.at[k - 1, f], face_in[k - 1].at[f], fc_recv.at[k - 1, f]
                ).wait()

    def whole(k, j):
        return wloc[j] + face_in[k - 1][facing[j]]

    def less_field(k, value_of):
        for j in range(SLOTS):
            near = spread_modes(mt[j], a_out[k] - al_near[k][beside[j]])
            part[j] = value_of(j) - near
        amplitude_done(k, range(2))
        for f in range(2):
            corr[f] = spread_modes(mt[slot_ref[0, f]], al_all[k][f])

    def assembled(j):
        return part[j] + corr[across[j]]

    def coarse_round(k, coef, sign, multiply, prepare):
        gather_send(k, coef, sign)
        multiply()
        faces_send(k)
        regions_send(k, gathered(k))
        prepare()
        solved(k)
        returned(k)
        faces_wait(k)
        less_field(k, lambda j: whole(k, j))

    def inner(total, left, right):
        return total + jnp.sum((left * right).reshape(FACE // 8, 8, NRHS), axis=0)

    def finish(total):
        return jnp.sum(total, axis=0, keepdims=True)

    zero8 = jnp.zeros((8, NRHS), f32)

    def coarse_matrix():
        finished(kdist.at[pl.ds(0, 7)], kd_recv.at[1])
        for r in range(NR):
            hi, lo = split(kdist[:, r].reshape(128, 128).T)
            khi[128 * r:128 * r + 128, :] = hi
            klo[128 * r:128 * r + 128, :] = lo

    def dual_start():
        for j in range(SLOTS):
            wloc[j] = gap_v[FACE * j:FACE * j + FACE, :] - product(dmat, j)
        hand_on(kdist, kd_send, kd_recv)

    def dirichlet():
        for j in range(SLOTS):
            wloc[j] = share[j] * product(emat, j)

    def unpacked(tile, b):
        before = jnp.where(lane_blk == (b + 8) % 16, tile, 0.0)
        after = jnp.where(lane_blk == (b + 9) % 16, tile, 0.0)
        return (
            jnp.where((lane_blk >= b - 1) & (lane_blk <= b + 1), tile, 0.0),
            pltpu.roll(before, 64, 1), pltpu.roll(after, 56, 1),
        )

    def coupling_matrix():
        finished(ldist.at[pl.ds(0, 7)], ld_recv.at[1])
        lmat[...] = jnp.zeros_like(lmat)
        for b in range(NBK):
            for g, at in enumerate((b + 16, b, b + 32, b + 15, b + 17)):
                if (g == 3 and b == 0) or (g == 4 and b == NBK - 1):
                    continue
                rows = slice(8 * at, 8 * at + 8)
                tile = ldist[b, g]
                for c, column in zip((128, 0, 256), unpacked(tile, b)):
                    lmat[rows, c:c + 128] = lmat[rows, c:c + 128] + column
        hi, lo = split(lmat[...])
        lhi[...] = hi
        llo[...] = lo

    def prepared():
        coupling_send()
        coarse_matrix()

    coarse_round(1, dcoef, -1, dual_start, prepared)
    for j in range(SLOTS):
        value = assembled(j)
        search[j] = value
        lower(j, share[j] * value)

    def owners_swap(i, k):
        for f in range(2):
            @pl.when(present[f])
            def _(f=f):
                send(
                    s3_out.at[k], t_in[i].at[f ^ 1], t_send.at[i, f], t_recv.at[i, f ^ 1], peer[f]
                )

            pending.append((present[f], s3_out.at[k], t_send.at[i, f]))

    def owners_coupled(i, k):
        for f in range(2):
            @pl.when(present[f])
            def _(f=f):
                finished(t_in[i].at[f], t_recv.at[i, f])
        pieces = []
        for tile in (t_in[i][0], s3_out[k], t_in[i][1]):
            hi = tile.astype(bf16).astype(f32)
            pieces.append(jnp.concatenate([hi, tile - hi], axis=0).astype(bf16))
        left = jnp.concatenate(pieces, axis=1)
        return add_up(dot(left, lhi[...]) + dot(left, llo[...]))

    lane_mode = lane_8 & 7
    six = jnp.zeros((6, NRHS), f32)

    def in_modes(x):
        return jnp.where(lane_mode < 6, x, 0.0)

    def row_sum(x):
        return jnp.sum(x, axis=1, keepdims=True)

    def search_coefficients():
        total = zero8
        for j in range(SLOTS):
            rows = slice(FACE * j, FACE * j + FACE)
            hi, lo = split(search[j])
            total = total + add_up(dot(m16[:, rows], hi) + dot(m16[:, rows], lo))
        return total

    def gather_with_sums(k, energy, cross, curvature, aside):
        extra = jnp.concatenate([six, finish(energy), finish(cross)], axis=0)
        one = jnp.zeros((1, NRHS), f32)
        aside = aside + jnp.concatenate([six, finish(curvature), one], axis=0)
        gather_send(k, dcoef, 1, extra, aside)

    def column_sums(i, k, gather, tiles, coupled):
        main, before, after = tiles
        beyond = zero8
        for t in range(NBK):
            beyond = beyond + jnp.where(lane_blk == (t + 4) % 16, s1_in[gather, t], 0.0)
        beyond = pltpu.roll(beyond, 96, 1)
        own, prior, later = s3_out[k], t_in[i][0], t_in[i][1]
        energy = row_sum(jnp.where(lane_mode == 6, main, 0.0) - in_modes(own * beyond))
        curvature = row_sum(
            jnp.where(lane_mode == 6, beyond, 0.0)
            + in_modes(
                own * (coupled[:, 128:256] - 2.0 * main)
                + prior * (coupled[:, 0:128] - 2.0 * before)
                + later * (coupled[:, 256:] - 2.0 * after)
            )
        )
        return jnp.where(lane_8 == 0, energy, 0.0) + jnp.where(lane_8 == 1, curvature, 0.0)

    def sums_start(out, arrived, k, stage):
        axis, me = (("region", region), ("block", block))[stage]
        all_to(
            axis, me, lambda to: out.at[stage], arrived.at[stage],
            st_send.at[k, stage], st_recv.at[k, stage],
        )
        arrived[stage, me] = out[stage]

    def sums_pass(out, arrived, k):
        await_all(arrived.at[0], st_recv.at[k, 0])
        out[1] = jnp.sum(arrived[0], axis=0)
        sums_start(out, arrived, k, 1)

    def sums_here(arrived, k):
        await_all(arrived.at[1], st_recv.at[k, 1])
        return arrived[1].reshape(128, 128).T

    gather_send(2, ecoef, 1)
    dirichlet()
    faces_send(2)
    aside = search_coefficients()
    regions_send(2, gathered(2))
    faces_wait(2)
    energy = zero8
    for j in range(SLOTS):
        value = whole(2, j)
        direc[j] = value
        lower(j, value)
        energy = inner(energy, share[j] * search[j], value)
    curvature = zero8
    for j in range(SLOTS):
        curvature = inner(curvature, direc[j], product(dmat, j))
    gather_with_sums(3, energy, zero8, curvature, aside)
    hand_on(ldist, ld_send, ld_recv)
    solved(2)
    owners_swap(0, 2)
    coupling_matrix()
    tiles = gathered(3)
    coupled = owners_coupled(0, 2)
    regions_send(
        3,
        (tiles[0] - coupled[:, 128:256], tiles[1] - coupled[:, 0:128], tiles[2] - coupled[:, 256:]),
    )
    c_out[0] = column_sums(0, 2, 3, tiles, coupled)
    sums_start(c_out, c_in, 6, 0)
    returned(2)
    less_field(2, lambda j: direc[j])
    for j in range(SLOTS):
        value = assembled(j)
        direc[j] = value
        lower(j, value)
    for j in range(SLOTS):
        value = product(dmat, j)
        wloc[j] = value
        field[j] = value
    faces_send(3)
    solved(3)
    sums_pass(c_out, c_in, 6)
    returned(3)
    faces_wait(3)
    less_field(3, lambda j: whole(3, j))
    sums = sums_here(c_in, 6)
    energy0 = sums[0:1, :]
    curvature0 = sums[1:2, :]
    step0 = energy0 / curvature0

    for j in range(SLOTS):
        value = search[j] - step0 * assembled(j)
        search[j] = value
        lower(j, share[j] * value)

    gather_send(4, ecoef, 1)
    dirichlet()
    faces_send(4)
    aside = search_coefficients()
    regions_send(4, gathered(4))
    faces_wait(4)
    energy = zero8
    cross = zero8
    for j in range(SLOTS):
        value = whole(4, j)
        wloc[j] = value
        lower(j, value)
        energy = inner(energy, share[j] * search[j], value)
        cross = inner(cross, value, field[j])
    curvature = zero8
    for j in range(SLOTS):
        curvature = inner(curvature, wloc[j], product(dmat, j))
    gather_with_sums(5, energy, cross, curvature, aside)
    solved(4)
    owners_swap(1, 4)
    tiles = gathered(5)
    coupled = owners_coupled(1, 4)
    crossed = row_sum(
        jnp.where(lane_mode == 7, tiles[0], 0.0)
        - in_modes(
            s3_out[4] * s2_out[3, 0] + t_in[1][0] * s2_out[3, 1] + t_in[1][1] * s2_out[3, 2]
        )
    )
    f_out[0] = column_sums(1, 4, 5, tiles, coupled) + jnp.where(lane_8 == 2, crossed, 0.0)
    sums_start(f_out, f_in, 7, 0)
    returned(4)
    less_field(4, lambda j: wloc[j])
    for j in range(SLOTS):
        search[j] = assembled(j)
    sums_pass(f_out, f_in, 7)
    sums = sums_here(f_in, 7)
    energy1 = sums[0:1, :]
    beta = energy1 / energy0
    curvature1 = sums[1:2, :] + 2.0 * beta * sums[2:3, :] + beta * beta * curvature0
    step1 = energy1 / curvature1
    first = step0 + step1 * beta
    for j in range(SLOTS):
        out_ref[FACE * j:FACE * j + FACE, :] = lam[j] + first * direc[j] + step1 * search[j]

    for condition, ref, sem in pending:
        if condition is None:
            finished(ref, sem)
        else:
            @pl.when(condition)
            def _(ref=ref, sem=sem):
                finished(ref, sem)


def body(
    gap_terms, rigid_loads, dual_matrix, dirichlet_matrix, rigid_modes, coarse_rows,
    face_slot, glue_sign,
):
    vmem = pl.BlockSpec(memory_space=pltpu.VMEM)
    hbm = pl.BlockSpec(memory_space=pl.ANY)
    V = pltpu.VMEM
    slots = (SLOTS, FACE, NRHS)
    scratch = [
        V((6, 1, NRHS), f32), V((6, 1, NL), f32), V((6, 1, NL), f32), V((1, NL), jnp.int32),
        V((NL, NL), bf16), V((NL, NL), bf16), V((NL, NRHS), f32), V((NL, NRHS), f32),
        V((16, NL), bf16), V((16, NL), bf16), V((SLOTS, FACE, 32), bf16), V((2, 8, NL), f32),
        V((6, 1, NL), f32), V((NR, 32, 96), bf16), V((NR, 8, 128), f32), V((NBK, NR, 8, 128), f32),
        V((NR * 128, 128), bf16), V((NR * 128, 128), bf16),
        V((96, NL), bf16), V((96, NL), bf16), V((SLOTS, 8, NRHS), f32),
        V((128, 128), f32), V((5, 8, 128), f32), V((NBK, 5, 8, 128), f32),
        V((384, 384), f32), V((384, 384), bf16), V((384, 384), bf16),
        tuple(V((2, 8, 128), f32) for _ in range(2)),
        V(slots, f32), V(slots, f32), V(slots, f32), V(slots, f32), V(slots, f32),
        V((NL, NRHS), bf16), V((SLOTS, 8, NRHS), f32), V((128, 128), f32), V((128, 128), f32),
        V((96, 1, 128), f32), V((NR, 96, 1, 128), f32), V((8, 128), f32), V((8, 128), f32),
        V((ROUNDS + 1, NBK, 8, 128), f32), V((ROUNDS + 1, NBK, 8, 128), f32),
        V((ROUNDS, 3, 8, 128), f32), V((ROUNDS, NR, 3, 8, 128), f32),
        V((ROUNDS, 8, 128), f32), V((ROUNDS, NBK, 8, 128), f32),
        V((ROUNDS, 8, 128), f32), tuple(V((5, 8, 128), f32) for _ in range(ROUNDS)),
        tuple(V((3, 8, 128), f32) for _ in range(ROUNDS)), V(slots, f32), V((3, FACE, NRHS), f32),
        V((4, 4, FACE, NRHS), f32), tuple(V((5, FACE, NRHS), f32) for _ in range(4)),
        V((3, 8, 128), f32), V((2, 16, 8, 128), f32),
        V((3, 8, 128), f32), V((2, 16, 8, 128), f32),
        pltpu.SemaphoreType.DMA((7,)), pltpu.SemaphoreType.DMA((2,)), pltpu.SemaphoreType.DMA((2,)),
        pltpu.SemaphoreType.DMA((2,)), pltpu.SemaphoreType.DMA((2,)),
        pltpu.SemaphoreType.DMA((2, 2)), pltpu.SemaphoreType.DMA((2, 2)),
        pltpu.SemaphoreType.DMA((2,)), pltpu.SemaphoreType.DMA((2,)),
        pltpu.SemaphoreType.DMA((ROUNDS + 3, 3)), pltpu.SemaphoreType.DMA((ROUNDS + 3, 3)),
        pltpu.SemaphoreType.DMA((ROUNDS, 4)), pltpu.SemaphoreType.DMA((ROUNDS, 4)),
        pltpu.SemaphoreType.DMA((4, 4)), pltpu.SemaphoreType.DMA((4, 4)),
    ]
    result = pl.pallas_call(
        kernel,
        out_shape=jax.ShapeDtypeStruct((NL, NRHS), f32),
        in_specs=[hbm] * 6 + [pl.BlockSpec(memory_space=pltpu.SMEM), hbm],
        out_specs=vmem,
        scratch_shapes=scratch,
        compiler_params=pltpu.CompilerParams(
            collective_id=0, has_side_effects=True, vmem_limit_bytes=60 * 1024 * 1024,
        ),
        cost_estimate=pl.CostEstimate(
            flops=5 * 2 * NL * NL * NRHS, bytes_accessed=12 * 1024 * 1024, transcendentals=0
        ),
    )(
        gap_terms, rigid_loads.transpose(0, 2, 1, 3), dual_matrix, dirichlet_matrix,
        rigid_modes.transpose(0, 2, 1, 3), coarse_rows.transpose(0, 2, 1, 3),
        face_slot, glue_sign,
    )
    return result[None, None]


def solution(mesh):
    matrix = P("region", "block", None, None)
    vector = P("region", "block", None)
    return jax.shard_map(
        body, mesh=mesh, in_specs=(matrix,) * 6 + (vector,) * 2, out_specs=matrix,
        check_vma=False,
    )
```
